512 devices in a mesh: ctx: 64 (over z, x), kvh: 8 (over y, core).
Axes of the slice: x: 4, y: 4, z: 16, core: 2. Of those that a mesh axis runs over, the one named last changes fastest.
Arguments:
- doc_lengths: int32 [64], replicated, may hold values from 1 to 384, 16384 in all
- queries: bfloat16 [2, 8192, 8192], P(None, ('ctx', 'kvh')), may hold values from -6 to 6
- key_matrix: bfloat16 [2, 8192, 1024], P(None, ('ctx', 'kvh')), may hold values from -6 to 6
- value_matrix: bfloat16 [2, 8192, 1024], P(None, ('ctx', 'kvh')), may hold values from -6 to 6
- forward_output: bfloat16 [2, 8192, 8192], P(None, ('ctx', 'kvh')), may hold values from -6 to 6
- output_cotangent: bfloat16 [2, 8192, 8192], P(None, ('ctx', 'kvh')), may hold values from -0.59765625 to 0.59765625
- log_normalizer_rows: float32 [2, 8192, 64], P(None, ('ctx', 'kvh')), may hold values from 1.5 to 3
Outputs:
- query_gradient: bfloat16 [2, 8192, 8192], P(None, 'ctx', 'kvh')
- key_gradient: bfloat16 [2, 8192, 1024], P(None, 'ctx', 'kvh')
- value_gradient: bfloat16 [2, 8192, 1024], P(None, 'ctx', 'kvh')
The draws below stay inside these ranges and needn't reach their ends.
Inputs may be any that keep to these rules, and one draw needn't show every extreme that they name: `doc_lengths`: the documents fill the pack of 16384 positions end to end; the longest has exactly 384 tokens.
All inputs are finite; a program needn't handle non-finite values.
Results may differ from the reference program's by a relative error of at most 0.0054.
Values may be sent and summed in bfloat16 or wider, within the bound.
No kernel may reach another device: no remote copies, remote signals or barrier semaphores. Data moves between devices by JAX's collectives and lax.ppermute only.
A program may use at most 64 MiB of HBM per device.

```python
import math
from functools import partial
import jax
import jax.numpy as jnp
import numpy as np
from jax import lax

QUERY_PER_GROUP = 8
HEAD_SIZE = 128
BLOCK_TOKENS = 128
LOOK = 3
KEY_VALUE_HEADS = 8
HQ = 64
HALF_TOKENS = 8192
DOCMAX = 384
DOCS = 64
N_CTX = 64


def block_scale(own_key, shape, split, least, high):
    def one(dim, parts):
        draws = jax.random.uniform(jax.random.fold_in(jax.random.fold_in(own_key, 6), dim), (parts,), jnp.float32, least / len(split), high / len(split))
        return jnp.repeat(jnp.exp(draws), shape[dim] // parts).reshape((-1,) + (1,) * (len(shape) - dim - 1))

    factor_of = one(*split[0])
    for cut in split[1:]:
        factor_of = factor_of * one(*cut)
    return factor_of


def profile(count, total, reach, skew):
    weights = [(1 << 20) // math.isqrt(grade ** skew) + 1 for grade in range(2, count + 1)]
    rest, holding = total - reach - (count - 1), [1] * (count - 1)
    while rest > 0:
        movable = [i for i in range(count - 1) if holding[i] < reach]
        mass, left = sum([weights[i] for i in movable]), rest
        for i in movable:
            extra = min(reach - holding[i], max(1, left * weights[i] // mass), rest)
            holding[i] = holding[i] + extra
            rest = rest - extra
    return np.array([reach] + holding)


def uneven_parts(own_key, amount, total, most, skew):
    if amount == 2:
        one = jax.random.randint(own_key, (), max(1, total - most), min(most, total - 1) + 1)
        return jnp.stack([one, total - one])
    tallies = jnp.asarray(profile(amount, total, most, skew), jnp.int32)
    twos = (amount - 1) // 2
    giver, sink = tallies[1:1 + 2 * twos:2], tallies[2:2 + 2 * twos:2]
    room = jnp.minimum(giver - 1, most - sink)
    moved = jax.random.randint(jax.random.fold_in(own_key, 1), (twos,), 0, 1 << 20) % (room + 1)
    tallies = tallies.at[1:1 + 2 * twos:2].set(giver - moved).at[2:2 + 2 * twos:2].set(sink + moved)
    return tallies[jax.random.permutation(jax.random.fold_in(own_key, 2), amount)]


def scatter_about(stream_key, extent, width, reach, pieces=(), held_as=jnp.bfloat16):
    values = jax.random.normal(stream_key, extent, jnp.float32) * width
    if len(pieces) > 0:
        values = block_scale(stream_key, extent, pieces, -0.22, 0.18) * values
    return jnp.clip(values, min=-reach, max=reach).astype(held_as)


def setup_inputs(seed: int = 0) -> dict:
    key_of = jax.random.split(jax.random.key(seed), 8)
    doc_lengths = uneven_parts(key_of[0], DOCS, 2 * N_CTX * BLOCK_TOKENS, DOCMAX, 1).astype(jnp.int32)
    queries = scatter_about(key_of[1], (2, HALF_TOKENS, HQ * HEAD_SIZE), 1.0, 6.0, ((1, 512),))
    key_matrix = scatter_about(key_of[2], (2, HALF_TOKENS, KEY_VALUE_HEADS * HEAD_SIZE), 1.0, 6.0, ((1, 512),))
    value_matrix = scatter_about(key_of[3], (2, HALF_TOKENS, KEY_VALUE_HEADS * HEAD_SIZE), 1.0, 6.0, ((1, 512),))
    forward_output = scatter_about(key_of[4], (2, HALF_TOKENS, HQ * HEAD_SIZE), 1.0, 6.0, ((1, 512),))
    output_cotangent = scatter_about(key_of[5], (2, HALF_TOKENS, HQ * HEAD_SIZE), 0.1, 0.59765625, ((1, 512),))
    log_normalizer_rows = jnp.clip(1.5 + 1.5 * jax.random.uniform(key_of[6], (2, HALF_TOKENS, HQ), jnp.float32) ** block_scale(key_of[6], (2, HALF_TOKENS, HQ), ((1, 512),), -0.2, 0.2), 1.5, 3.0)
    return dict(doc_lengths=doc_lengths, queries=queries, key_matrix=key_matrix, value_matrix=value_matrix, forward_output=forward_output, output_cotangent=output_cotangent, log_normalizer_rows=log_normalizer_rows)


def spread_rows(array):
    upper_half = array[1].reshape((N_CTX, BLOCK_TOKENS) + array.shape[2:])[::-1].reshape(array.shape[1:])
    return jnp.concatenate([array[0], upper_half], axis=0)


def fold_back_rows(array):
    half_len = array.shape[0] // 2
    upper_half = array[half_len:].reshape((N_CTX, BLOCK_TOKENS) + array.shape[1:])[::-1].reshape((half_len,) + array.shape[1:])
    return jnp.stack([array[:half_len], upper_half])


def tile_grads(query_tile, grad_tile, norm_tile, delta_tile, key_tile, value_tile, allowed):
    inv_root = HEAD_SIZE ** -0.5
    scores = jnp.einsum("qhgd,khd->hgqk", query_tile, key_tile) * inv_root
    weights = jnp.where(allowed[None, None], jnp.exp(scores - norm_tile[:, :, :, None]), 0.0)
    weight_bf = lax.optimization_barrier(weights.astype(jnp.bfloat16)).astype(jnp.float32)
    value_gradient = jnp.einsum("hgqk,qhgd->khd", weight_bf, grad_tile)
    weight_grad = jnp.einsum("qhgd,khd->hgqk", grad_tile, value_tile)
    score_grad = weights * (weight_grad - delta_tile[:, :, :, None])
    score_bf = lax.optimization_barrier(score_grad.astype(jnp.bfloat16)).astype(jnp.float32)
    query_gradient = jnp.einsum("hgqk,khd->qhgd", score_bf, key_tile) * inv_root
    key_gradient = jnp.einsum("hgqk,qhgd->khd", score_bf, query_tile) * inv_root
    return query_gradient, key_gradient, value_gradient


def empty_grads():
    return (jnp.zeros((BLOCK_TOKENS, KEY_VALUE_HEADS, QUERY_PER_GROUP, HEAD_SIZE), jnp.float32), jnp.zeros((BLOCK_TOKENS, KEY_VALUE_HEADS, HEAD_SIZE), jnp.float32), jnp.zeros((BLOCK_TOKENS, KEY_VALUE_HEADS, HEAD_SIZE), jnp.float32))


def reference(doc_lengths, queries, key_matrix, value_matrix, forward_output, output_cotangent, log_normalizer_rows):
    sequence_length = 2 * N_CTX * BLOCK_TOKENS
    padding_length = LOOK * BLOCK_TOKENS
    query_full = spread_rows(queries).astype(jnp.float32).reshape(sequence_length, KEY_VALUE_HEADS, QUERY_PER_GROUP, HEAD_SIZE)
    gradient_full = spread_rows(output_cotangent).astype(jnp.float32).reshape(sequence_length, KEY_VALUE_HEADS, QUERY_PER_GROUP, HEAD_SIZE)
    output_full = spread_rows(forward_output).astype(jnp.float32).reshape(sequence_length, KEY_VALUE_HEADS, QUERY_PER_GROUP, HEAD_SIZE)
    delta_all = jnp.sum(gradient_full * output_full, axis=-1)
    norm_full = spread_rows(log_normalizer_rows).reshape(sequence_length, KEY_VALUE_HEADS, QUERY_PER_GROUP)
    key_full = jnp.pad(spread_rows(key_matrix).astype(jnp.float32).reshape(sequence_length, KEY_VALUE_HEADS, HEAD_SIZE), ((padding_length, 0), (0, 0), (0, 0)))
    value_full = jnp.pad(spread_rows(value_matrix).astype(jnp.float32).reshape(sequence_length, KEY_VALUE_HEADS, HEAD_SIZE), ((padding_length, 0), (0, 0), (0, 0)))
    doc_ends = jnp.cumsum(doc_lengths)
    position = jnp.arange(sequence_length, dtype=jnp.int32)
    doc_ids = jnp.sum((doc_ends[None, :] <= position[:, None]).astype(jnp.int32), axis=1)
    key_docs = jnp.concatenate([jnp.full((padding_length,), -1, jnp.int32), doc_ids])
    key_pos = jnp.arange(sequence_length + padding_length, dtype=jnp.int32) - padding_length

    def block_step(grad_sums, block_id):
        key_gradient_totals, value_gradient_totals = grad_sums
        row_start = block_id * BLOCK_TOKENS
        query_tile = lax.dynamic_slice_in_dim(query_full, row_start, BLOCK_TOKENS, 0)
        grad_tile = lax.dynamic_slice_in_dim(gradient_full, row_start, BLOCK_TOKENS, 0)
        norm_tile = jnp.transpose(lax.dynamic_slice_in_dim(norm_full, row_start, BLOCK_TOKENS, 0), (1, 2, 0))
        delta_tile = jnp.transpose(lax.dynamic_slice_in_dim(delta_all, row_start, BLOCK_TOKENS, 0), (1, 2, 0))
        query_docs = lax.dynamic_slice_in_dim(doc_ids, row_start, BLOCK_TOKENS, 0)
        query_pos = row_start + jnp.arange(BLOCK_TOKENS, dtype=jnp.int32)
        query_total = jnp.zeros((BLOCK_TOKENS, KEY_VALUE_HEADS, QUERY_PER_GROUP, HEAD_SIZE), jnp.float32)
        for lookback in range(LOOK + 1):
            key_start = row_start + (LOOK - lookback) * BLOCK_TOKENS
            key_tile = lax.dynamic_slice_in_dim(key_full, key_start, BLOCK_TOKENS, 0)
            value_tile = lax.dynamic_slice_in_dim(value_full, key_start, BLOCK_TOKENS, 0)
            tile_docs = lax.dynamic_slice_in_dim(key_docs, key_start, BLOCK_TOKENS, 0)
            tile_pos = lax.dynamic_slice_in_dim(key_pos, key_start, BLOCK_TOKENS, 0)
            same_doc = query_docs[:, None] == tile_docs[None, :]
            allowed = same_doc & (tile_pos[None, :] <= query_pos[:, None])
            compute = partial(tile_grads, query_tile, grad_tile, norm_tile, delta_tile, key_tile, value_tile, allowed)
            query_part, key_part, value_part = lax.cond(jnp.any(same_doc), compute, empty_grads)
            query_total = query_total + query_part
            key_gradient_totals = lax.dynamic_update_slice_in_dim(key_gradient_totals, lax.dynamic_slice_in_dim(key_gradient_totals, key_start, BLOCK_TOKENS, 0) + key_part, key_start, 0)
            value_gradient_totals = lax.dynamic_update_slice_in_dim(value_gradient_totals, lax.dynamic_slice_in_dim(value_gradient_totals, key_start, BLOCK_TOKENS, 0) + value_part, key_start, 0)
        return (key_gradient_totals, value_gradient_totals), query_total

    initial_totals = (jnp.zeros((sequence_length + padding_length, KEY_VALUE_HEADS, HEAD_SIZE), jnp.float32), jnp.zeros((sequence_length + padding_length, KEY_VALUE_HEADS, HEAD_SIZE), jnp.float32))
    (key_gradient_totals, value_gradient_totals), query_gradient_totals = lax.scan(block_step, initial_totals, jnp.arange(2 * N_CTX, dtype=jnp.int32))
    query_gradient = fold_back_rows(query_gradient_totals.reshape(sequence_length, KEY_VALUE_HEADS * QUERY_PER_GROUP * HEAD_SIZE).astype(jnp.bfloat16))
    key_gradient = fold_back_rows(key_gradient_totals[padding_length:].reshape(sequence_length, KEY_VALUE_HEADS * HEAD_SIZE).astype(jnp.bfloat16))
    value_gradient = fold_back_rows(value_gradient_totals[padding_length:].reshape(sequence_length, KEY_VALUE_HEADS * HEAD_SIZE).astype(jnp.bfloat16))
    return query_gradient, key_gradient, value_gradient
```

```python
import jax
import jax.numpy as jnp
from jax import lax
from jax.experimental import pallas as pl
from jax.experimental.pallas import tpu as pltpu
from jax.sharding import PartitionSpec as P

GROUP = 8
HEAD = 128
BLOCK = 128
DOCS = 64
INV_ROOT = HEAD**-0.5
LOG2E = 1.4426950408889634
MASKED = -1e30
BF = jnp.bfloat16
F32 = jnp.float32


def call(kernel, outs, n_in, smem=(), scratch=()):
    specs = [
        pl.BlockSpec(memory_space=pltpu.SMEM if i in smem else pltpu.VMEM) for i in range(n_in)
    ]
    return pl.pallas_call(
        kernel,
        out_shape=[jax.ShapeDtypeStruct(*o) for o in outs],
        in_specs=specs,
        out_specs=[pl.BlockSpec(memory_space=pltpu.VMEM)] * len(outs),
        scratch_shapes=list(scratch),
        compiler_params=pltpu.CompilerParams(vmem_limit_bytes=40 * 1024 * 1024),
    )


def two_terms(x):
    high = x.astype(BF)
    return high, (x - high.astype(F32)).astype(BF)


def pack_small(key_ref, value_ref, out_ref, grad_ref, norm_ref, packed_ref):
    heads = grad_ref.shape[2] // HEAD
    lane = lax.broadcasted_iota(jnp.int32, (16, heads), 1)
    for half in range(2):
        rows = pl.ds(half * 16, 16)
        delta = jnp.zeros((16, heads), F32)
        for n in range(heads):
            cols = pl.ds(n * HEAD, HEAD)
            product = out_ref[half, :, cols].astype(F32) * grad_ref[half, :, cols].astype(F32)
            delta = jnp.where(lane == n, jnp.sum(product, axis=1, keepdims=True), delta)
        stats = jnp.concatenate([*two_terms(norm_ref[half]), *two_terms(delta)], axis=1)
        for j in range(8):
            cols = pl.ds(j * HEAD, HEAD)
            packed_ref[j, rows, 0:128] = key_ref[half, :, cols]
            packed_ref[j, rows, 128:256] = value_ref[half, :, cols]
            packed_ref[j, rows, 256:512] = stats


def pack_large(query_ref, grad_ref, packed_ref):
    for half in range(2):
        rows = pl.ds(half * 16, 16)
        for j in range(8):
            cols = pl.ds(j * 1024, 1024)
            packed_ref[j, rows, 0:1024] = query_ref[half, :, cols]
            packed_ref[j, rows, 1024:2048] = grad_ref[half, :, cols]


def unpack_small(length_ref, packed_ref, low_ref, high_ref, stat_ref, start_ref, turned):
    ctx = lax.axis_index("ctx")
    kvh = lax.axis_index("kvh")
    for half, kv_ref in enumerate((low_ref, high_ref)):
        rows = pl.ds(half * 16, 16)
        kv_ref[...] = packed_ref[:, rows, 0:256].reshape(BLOCK, 256)
        stats = packed_ref[:, rows, 256:512].reshape(BLOCK, 256).astype(F32)
        turned[...] = stats.T
        first = pl.multiple_of(kvh * GROUP, GROUP)
        for s, factor in enumerate((LOG2E, 1.0)):
            total = (
                turned[pl.ds(s * 128 + first, GROUP), :]
                + turned[pl.ds(s * 128 + 64 + first, GROUP), :]
            )
            stat_ref[half, s] = total * factor
    row = lax.broadcasted_iota(jnp.int32, (8, BLOCK), 0)
    base = jnp.where(row == 0, ctx, 127 - ctx) * BLOCK
    position = base + lax.broadcasted_iota(jnp.int32, (8, BLOCK), 1)
    start = jnp.zeros((8, BLOCK), jnp.int32)
    end = jnp.int32(0)
    for j in range(DOCS):
        end = end + length_ref[j]
        start = jnp.where(position >= end, end, start)
    start_ref[...] = start - base


def pair_up(low_ref, high_ref, low1_ref, high1_ref, even_ref, odd_ref, pair1_ref):
    ctx = lax.axis_index("ctx")
    even = lax.rem(ctx, 2) == 0
    before_high = jnp.where(ctx == 63, low_ref[...], high1_ref[...])
    before_low = low1_ref[...]
    low, high = low_ref[...], high_ref[...]
    even_ref[0] = jnp.where(even, low, high)
    even_ref[1] = jnp.where(even, before_low, before_high)
    odd_ref[0] = jnp.where(even, high, low)
    odd_ref[1] = jnp.where(even, before_high, before_low)
    pair1_ref[0] = before_low
    pair1_ref[1] = before_high


def dot(a, b, contract):
    return lax.dot_general(a, b, ((contract[:1], contract[1:]), ((), ())), preferred_element_type=F32)


def gradients(
    rows_ref, low_ref, high_ref, pair1_ref, even_ref, odd_ref, stat_ref, start_ref,
    query_out, far_ref, near_ref, turned,
):
    ctx = lax.axis_index("ctx")
    even = lax.rem(ctx, 2) == 0
    key_at = lax.broadcasted_iota(jnp.int32, (BLOCK, BLOCK), 0)
    row_at = lax.broadcasted_iota(jnp.int32, (BLOCK, BLOCK), 1)
    for half, own_ref in enumerate((low_ref, high_ref)):
        start = start_ref[half : half + 1, :]
        takes_even = even if half == 0 else jnp.logical_not(even)
        for far in (True, False):
            if far:
                tiles = [jnp.where(takes_even, even_ref[s], odd_ref[s]) for s in range(2)]
            else:
                tiles = [own_ref[...], pair1_ref[half]]
            allowed = [key_at - BLOCK * (s + 2 * far) >= start for s in range(2)]
            if not far:
                allowed[0] = allowed[0] & (key_at <= row_at)
            bias = jnp.concatenate([jnp.where(a, 0.0, MASKED) for a in allowed], axis=0)
            bias = jnp.concatenate([bias, bias], axis=1)
            keys = jnp.concatenate([t[:, :HEAD] for t in tiles], axis=0)
            values = jnp.concatenate([t[:, HEAD:] for t in tiles], axis=0)
            keys_turned = keys.T
            key_total = jnp.zeros((2 * BLOCK, HEAD), F32)
            value_total = jnp.zeros((2 * BLOCK, HEAD), F32)
            for g in range(0, GROUP, 2):
                def head_pair(offset):
                    return jnp.concatenate(
                        [
                            rows_ref[
                                :, half * 16 : half * 16 + 16,
                                offset + n * HEAD : offset + (n + 1) * HEAD,
                            ].reshape(BLOCK, HEAD)
                            for n in (g, g + 1)
                        ],
                        axis=0,
                    )

                query, grad = head_pair(0), head_pair(1024)
                norm, delta = (
                    jnp.concatenate([stat_ref[half, s, n : n + 1, :] for n in (g, g + 1)], axis=1)
                    for s in range(2)
                )
                scores = dot(keys, query, (1, 1))
                weights = jnp.exp2(scores * (INV_ROOT * LOG2E) - norm + bias)
                weight_grad = dot(values, grad, (1, 1))
                score_grad = (weights * (weight_grad - delta)).astype(BF)
                value_total += dot(weights.astype(BF), grad, (1, 0))
                key_total += dot(score_grad, query, (1, 0))
                query_part = dot(keys_turned, score_grad, (1, 0))
                if far:
                    turned[:, g * HEAD : (g + 2) * HEAD] = query_part
                else:
                    query_part = (query_part + turned[:, g * HEAD : (g + 2) * HEAD]) * INV_ROOT
                    for n in range(2):
                        query_out[half, :, (g + n) * HEAD : (g + n + 1) * HEAD] = (
                            query_part[:, n * HEAD : (n + 1) * HEAD].T.astype(BF)
                        )
            key_total = key_total * INV_ROOT
            if far:
                slot = jnp.where(takes_even, 0, 1)
                for s in range(2):
                    part = slice(s * BLOCK, (s + 1) * BLOCK)
                    far_ref[slot, s, :, :HEAD] = key_total[part].astype(BF)
                    far_ref[slot, s, :, HEAD:] = value_total[part].astype(BF)
            else:
                for s in range(2):
                    part = slice(s * BLOCK, (s + 1) * BLOCK)
                    near_ref[half, s, :, :HEAD] = key_total[part]
                    near_ref[half, s, :, HEAD:] = value_total[part]


def add_far(near_ref, even_ref, odd_ref, own_ref, low_ref, high_ref, fold_ref):
    even = lax.rem(lax.axis_index("ctx"), 2) == 0
    for half, send_ref in enumerate((low_ref, high_ref)):
        takes_even = even if half == 0 else jnp.logical_not(even)
        got = [
            jnp.where(takes_even, even_ref[s].astype(F32), odd_ref[s].astype(F32)) for s in range(2)
        ]
        own_ref[half] = near_ref[half, 0] + got[0]
        before = near_ref[half, 1] + got[1]
        send_ref[...] = before.astype(BF)
        if half == 1:
            fold_ref[...] = before


def add_near(own_ref, fold_ref, low_ref, high_ref, key_out, value_out):
    at_fold = lax.axis_index("ctx") == 63
    for half, got_ref in enumerate((low_ref, high_ref)):
        got = got_ref[...].astype(F32)
        if half == 0:
            got = jnp.where(at_fold, fold_ref[...], got)
        total = own_ref[half] + got
        key_out[half] = total[:, :HEAD].astype(BF)
        value_out[half] = total[:, HEAD:].astype(BF)


def body(lengths, queries, keys, values, outputs, grads, norms):
    last = 2 * lax.axis_size("ctx") - 1

    def owner(p):
        return min(p, last - p)

    up = [(i, i + 1) for i in range(last // 2)]
    down = [(j, i) for i, j in up]
    skips = [[(owner(p), owner(p + 2)) for p in range(first, last - 1, 2)] for first in range(2)]
    backs = [[(j, i) for i, j in skip] for skip in skips]

    def by_head(x):
        return lax.all_to_all(x, "kvh", split_axis=0, concat_axis=0, tiled=True)

    (small,) = call(pack_small, [((8, 32, 512), BF)], 5)(keys, values, outputs, grads, norms)
    small = by_head(small)
    (large,) = call(pack_large, [((8, 32, 2048), BF)], 2)(queries, grads)
    large = by_head(large)
    tile, pair = ((BLOCK, 256), BF), ((2, BLOCK, 256), BF)
    low, high, stats, starts = call(
        unpack_small,
        [tile, tile, ((2, 2, GROUP, BLOCK), F32), ((8, BLOCK), jnp.int32)],
        2,
        smem=(0,),
        scratch=[pltpu.VMEM((256, BLOCK), F32)],
    )(lengths, small)
    low1 = lax.ppermute(low, "ctx", up)
    high1 = lax.ppermute(high, "ctx", down)
    even, odd, pair1 = call(pair_up, [pair, pair, pair], 4)(low, high, low1, high1)
    even, odd = (lax.ppermute(x, "ctx", skip) for x, skip in zip((even, odd), skips))
    query_grad, far, near = call(
        gradients,
        [
            ((2, BLOCK, 1024), BF),
            ((2, 2, BLOCK, 256), BF),
            ((2, 2, BLOCK, 256), F32),
        ],
        8,
        scratch=[pltpu.VMEM((HEAD, 1024), F32)],
    )(large, low, high, pair1, even, odd, stats, starts)
    even, odd = (lax.ppermute(far[s], "ctx", backs[s]) for s in range(2))
    own, low, high, fold = call(
        add_far, [((2, BLOCK, 256), F32), tile, tile, ((BLOCK, 256), F32)], 3
    )(near, even, odd)
    low = lax.ppermute(low, "ctx", down)
    high = lax.ppermute(high, "ctx", up)
    key_grad, value_grad = call(add_near, [((2, BLOCK, HEAD), BF)] * 2, 4)(own, fold, low, high)
    return query_grad, key_grad, value_grad


def solution(mesh):
    rows = P(None, ("ctx", "kvh"), None)
    heads = P(None, "ctx", "kvh")
    return jax.shard_map(
        body,
        mesh=mesh,
        in_specs=(P(),) + (rows,) * 6,
        out_specs=(heads,) * 3,
        check_vma=False,
    )
```

```python
import jax
import jax.numpy as jnp
from jax import lax
from jax.experimental import pallas as pl
from jax.experimental.pallas import tpu as pltpu
from jax.sharding import PartitionSpec as P

GROUP = 8
HEAD = 128
BLOCK = 128
DOCS = 64
INV_ROOT = HEAD**-0.5
LOG2E = 1.4426950408889634
MASKED = -1e30
ALL = 60
BF = jnp.bfloat16
F32 = jnp.float32


def call(kernel, outs, n_in, smem=(), scratch=(), raw=False):
    place = pltpu.HBM if raw else pltpu.VMEM
    specs = [pl.BlockSpec(memory_space=pltpu.SMEM if i in smem else place) for i in range(n_in)]
    return pl.pallas_call(
        kernel,
        out_shape=[jax.ShapeDtypeStruct(*o) for o in outs],
        in_specs=specs,
        out_specs=[pl.BlockSpec(memory_space=pltpu.VMEM)] * len(outs),
        scratch_shapes=list(scratch),
        compiler_params=pltpu.CompilerParams(vmem_limit_bytes=(ALL if raw else 40) * 1024 * 1024),
    )


def fetch(sources, targets, sems):
    copies = [
        pltpu.make_async_copy(source, target, sems.at[i])
        for i, (source, target) in enumerate(zip(sources, targets))
    ]
    for copy in copies:
        copy.start()
    for copy in copies:
        copy.wait()


def two_terms(x):
    high = x.astype(BF)
    return high, (x - high.astype(F32)).astype(BF)


def pack_small(key_raw, value_raw, packed_ref, key_ref, value_ref, sems):
    fetch((key_raw, value_raw), (key_ref, value_ref), sems)
    for half in range(2):
        rows = pl.ds(half * 16, 16)
        for j in range(8):
            cols = pl.ds(j * HEAD, HEAD)
            packed_ref[j, rows, :HEAD] = key_ref[half, :, cols]
            packed_ref[j, rows, HEAD:] = value_ref[half, :, cols]


def pack_large(length_ref, *refs):
    packed_ref, start_ref, sems = refs[4], refs[5], refs[10]
    fetch(refs[:4], refs[6:10], sems)
    query_ref, grad_ref, out_ref, norm_ref = refs[6:10]
    heads = grad_ref.shape[2] // HEAD
    lane = lax.broadcasted_iota(jnp.int32, (16, heads), 1)
    source = lax.broadcasted_iota(jnp.int32, (4 * heads, HEAD), 0)
    target = lax.broadcasted_iota(jnp.int32, (4 * heads, HEAD), 1)
    offset = source - (lax.div(target, GROUP) * heads + lax.rem(target, GROUP))
    stats = []
    for half in range(2):
        delta = jnp.zeros((16, heads), F32)
        for n in range(heads):
            cols = pl.ds(n * HEAD, HEAD)
            product = out_ref[half, :, cols].astype(F32) * grad_ref[half, :, cols].astype(F32)
            delta = jnp.where(lane == n, jnp.sum(product, axis=1, keepdims=True), delta)
        stats.append(jnp.concatenate([*two_terms(norm_ref[half]), *two_terms(delta)], axis=1))
    stats = jnp.concatenate(stats, axis=0)
    for j in range(8):
        pick = jnp.where((offset == j * GROUP) & (target < 4 * GROUP), 1.0, 0.0).astype(BF)
        packed_ref[j, :, 2048:] = dot(stats, pick, (1, 0)).astype(BF)
        for half in range(2):
            rows = pl.ds(half * 16, 16)
            cols = pl.ds(j * 1024, 1024)
            packed_ref[j, rows, 0:1024] = query_ref[half, :, cols]
            packed_ref[j, rows, 1024:2048] = grad_ref[half, :, cols]
    ctx = lax.axis_index("ctx")
    row = lax.broadcasted_iota(jnp.int32, (8, BLOCK), 0)
    base = jnp.where(row == 0, ctx, 127 - ctx) * BLOCK
    position = base + lax.broadcasted_iota(jnp.int32, (8, BLOCK), 1)
    start = jnp.zeros((8, BLOCK), jnp.int32)
    end = jnp.int32(0)
    for j in range(DOCS):
        end = end + length_ref[j]
        start = jnp.where(position >= end, end, start)
    start_ref[...] = start - base


def unpack_small(packed_ref, even_ref, odd_ref):
    even = lax.rem(lax.axis_index("ctx"), 2) == 0
    low, high = (packed_ref[:, h : h + 16, :].reshape(BLOCK, 256) for h in (0, 16))
    even_ref[...] = jnp.where(even, low, high)
    odd_ref[...] = jnp.where(even, high, low)


def dot(a, b, contract):
    return lax.dot_general(a, b, ((contract[:1], contract[1:]), ((), ())), preferred_element_type=F32)


def pair_up(even_ref, odd_ref, before_even, before_odd, even_out, odd_out):
    even_out[0] = even_ref[...]
    even_out[1] = before_even[...]
    odd_out[0] = odd_ref[...]
    odd_out[1] = before_odd[...]


def two_tiles(rows_ref, stat_ref, start_ref, half, first, tiles, put_query):
    key_at = lax.broadcasted_iota(jnp.int32, (BLOCK, BLOCK), 0)
    row_at = lax.broadcasted_iota(jnp.int32, (BLOCK, BLOCK), 1)
    start = start_ref[half : half + 1, :]
    allowed = [key_at - BLOCK * (first + s) >= start for s in range(2)]
    if first == 0:
        allowed[0] = allowed[0] & (key_at <= row_at)
    bias = jnp.concatenate([jnp.where(a, 0.0, MASKED) for a in allowed], axis=0)
    bias = jnp.concatenate([bias, bias], axis=1)
    keys = jnp.concatenate([t[:, :HEAD] for t in tiles], axis=0)
    values = jnp.concatenate([t[:, HEAD:] for t in tiles], axis=0)
    keys_turned = keys.T
    key_total = jnp.zeros((2 * BLOCK, HEAD), F32)
    value_total = jnp.zeros((2 * BLOCK, HEAD), F32)
    rows = slice(half * 16, half * 16 + 16)
    for g in range(0, GROUP, 2):

        def head_pair(offset):
            columns = [slice(offset + n * HEAD, offset + (n + 1) * HEAD) for n in (g, g + 1)]
            return jnp.concatenate([rows_ref[:, rows, c].reshape(BLOCK, HEAD) for c in columns], 0)

        query, grad = head_pair(0), head_pair(1024)
        norm, delta = (
            jnp.concatenate([stat_ref[half, s, n : n + 1, :] for n in (g, g + 1)], axis=1)
            for s in range(2)
        )
        scores = dot(keys, query, (1, 1))
        weights = jnp.exp2(scores * (INV_ROOT * LOG2E) - norm + bias)
        weight_grad = dot(values, grad, (1, 1))
        score_grad = (weights * (weight_grad - delta)).astype(BF)
        value_total += dot(weights.astype(BF), grad, (1, 0))
        key_total += dot(score_grad, query, (1, 0))
        put_query(g, dot(keys_turned, score_grad, (1, 0)))
    return key_total * INV_ROOT, value_total


def near_gradients(
    rows_ref, even_ref, odd_ref, before_even, before_odd, start_ref,
    turned, own_out, near_out, stat_ref, stat_turned,
):
    even = lax.rem(lax.axis_index("ctx"), 2) == 0
    for half in range(2):
        stats = rows_ref[:, half * 16 : half * 16 + 16, 2048:2176].reshape(BLOCK, HEAD)
        stat_turned[...] = stats.astype(F32).T
        stat_ref[half, 0] = (stat_turned[0:8, :] + stat_turned[8:16, :]) * LOG2E
        stat_ref[half, 1] = stat_turned[16:24, :] + stat_turned[24:32, :]
        is_even = even if half == 0 else jnp.logical_not(even)
        tiles = [
            jnp.where(is_even, even_ref[...], odd_ref[...]),
            jnp.where(is_even, before_even[...], before_odd[...]),
        ]

        def put(g, part):
            turned[half, :, g * HEAD : (g + 2) * HEAD] = part

        key_total, value_total = two_tiles(
            rows_ref, stat_ref, start_ref, half, 0, tiles, put
        )
        own_out[half, :, :HEAD] = key_total[:BLOCK]
        own_out[half, :, HEAD:] = value_total[:BLOCK]
        near_out[half, :, :HEAD] = key_total[BLOCK:].astype(BF)
        near_out[half, :, HEAD:] = value_total[BLOCK:].astype(BF)


def far_gradients(
    rows_ref, before_even, before_odd, stat_ref, start_ref, turned, near_ref,
    query_out, send_ref,
):
    ctx = lax.axis_index("ctx")
    member = lax.rem(ctx, 8)
    even = lax.rem(ctx, 2) == 0
    for half in range(2):
        is_even = even if half == 0 else jnp.logical_not(even)
        tiles = [jnp.where(is_even, before_even[s], before_odd[s]) for s in range(2)]

        def put(g, part):
            part = (part + turned[half, :, g * HEAD : (g + 2) * HEAD]) * INV_ROOT
            for n in range(2):
                query_out[half, :, (g + n) * HEAD : (g + n + 1) * HEAD] = (
                    part[:, n * HEAD : (n + 1) * HEAD].T.astype(BF)
                )

        key_total, value_total = two_tiles(
            rows_ref, stat_ref, start_ref, half, 2, tiles, put
        )
        for back in (1, 2, 3):
            slot = lax.rem(member + (back if half else 8 - back), 8)
            if back == 1:
                send_ref[slot] = near_ref[half]
            else:
                part = slice((back - 2) * BLOCK, (back - 1) * BLOCK)
                send_ref[slot, :, :HEAD] = key_total[part].astype(BF)
                send_ref[slot, :, HEAD:] = value_total[part].astype(BF)
    for apart in (0, 4):
        send_ref[lax.rem(member + apart, 8)] = jnp.zeros((BLOCK, 2 * HEAD), BF)


def add_group(own_ref, got_ref, sum_ref, pass_ref):
    member = lax.rem(lax.axis_index("ctx"), 8)
    zero = jnp.zeros((BLOCK, 2 * HEAD), F32)
    low, high, other = own_ref[0], own_ref[1], zero
    for s in range(8):
        got = got_ref[s].astype(F32)
        apart = lax.rem(s - member + 8, 8)
        from_low = (apart >= 1) & (apart <= 3)
        from_high = apart >= 5
        low = low + jnp.where(from_low & (s > member), got, 0.0)
        high = high + jnp.where(from_high & (s < member), got, 0.0)
        other = other + jnp.where((from_low & (s < member)) | (from_high & (s > member)), got, 0.0)
    sum_ref[0] = low
    sum_ref[1] = high
    pass_ref[...] = other.astype(BF)


def add_rest(sum_ref, got_ref, key_out, value_out):
    odd = lax.rem(lax.div(lax.axis_index("ctx"), 4), 2) == 1
    got = got_ref[...].astype(F32)
    for half in range(2):
        pick = odd if half == 0 else jnp.logical_not(odd)
        total = sum_ref[half] + jnp.where(pick, got, 0.0)
        key_out[half] = total[:, :HEAD].astype(BF)
        value_out[half] = total[:, HEAD:].astype(BF)


def between_groups():
    pairs = []
    for x in range(4):
        pairs += [(4 * z + x, 4 * (z + 2) + x) for z in range(0, 13, 2)]
        pairs += [(4 * z + x, 4 * (z - 2) + x) for z in range(3, 16, 2)]
        pairs += [(56 + x, 63 - x)]
    return pairs


def body(lengths, queries, keys, values, outputs, grads, norms):
    last = 2 * lax.axis_size("ctx") - 1

    def owner(p):
        return min(p, last - p)

    def later(first, back):
        return [(owner(p), owner(p + back)) for p in range(first, last + 1 - back, 2)]

    groups = [[8 * m + j for j in range(8)] for m in range(8)]

    def by_head(x):
        return lax.all_to_all(x, "kvh", split_axis=0, concat_axis=0, tiled=True)

    (small,) = call(
        pack_small,
        [((8, 32, 256), BF)],
        2,
        scratch=[pltpu.VMEM((2, 16, 1024), BF)] * 2 + [pltpu.SemaphoreType.DMA((2,))],
        raw=True,
    )(keys, values)
    small = by_head(small)
    large, starts = call(
        pack_large,
        [((8, 32, 2176), BF), ((8, BLOCK), jnp.int32)],
        5,
        smem=(0,),
        scratch=[pltpu.VMEM((2, 16, 8192), BF)] * 3
        + [pltpu.VMEM((2, 16, 64), F32), pltpu.SemaphoreType.DMA((4,))],
        raw=True,
    )(lengths, queries, grads, outputs, norms)
    large = by_head(large)
    tile = ((BLOCK, 256), BF)
    even, odd = call(unpack_small, [tile, tile], 1)(small)
    before_odd = lax.ppermute(even, "ctx", later(0, 1))
    before_even = lax.ppermute(odd, "ctx", later(1, 1))
    pair = ((2, BLOCK, 256), BF)
    even_pair, odd_pair = call(pair_up, [pair, pair], 4)(even, odd, before_even, before_odd)
    even_pair = lax.ppermute(even_pair, "ctx", later(0, 2))
    odd_pair = lax.ppermute(odd_pair, "ctx", later(1, 2))
    turned, own, near, stats = call(
        near_gradients,
        [
            ((2, HEAD, 1024), F32),
            ((2, BLOCK, 256), F32),
            pair,
            ((2, 2, GROUP, BLOCK), F32),
        ],
        6,
        scratch=[pltpu.VMEM((HEAD, BLOCK), F32)],
    )(large, even, odd, before_even, before_odd, starts)
    query_grad, sent = call(
        far_gradients, [((2, BLOCK, 1024), BF), ((8, BLOCK, 256), BF)], 7
    )(large, even_pair, odd_pair, stats, starts, turned, near)
    got = lax.all_to_all(
        sent, "ctx", split_axis=0, concat_axis=0, tiled=True, axis_index_groups=groups
    )
    sums, passed = call(add_group, [((2, BLOCK, 256), F32), tile], 2)(own, got)
    passed = lax.ppermute(passed, "ctx", between_groups())
    key_grad, value_grad = call(add_rest, [((2, BLOCK, HEAD), BF)] * 2, 2)(sums, passed)
    return query_grad, key_grad, value_grad


def solution(mesh):
    rows = P(None, ("ctx", "kvh"), None)
    heads = P(None, "ctx", "kvh")
    return jax.shard_map(
        body,
        mesh=mesh,
        in_specs=(P(),) + (rows,) * 6,
        out_specs=(heads,) * 3,
        check_vma=False,
    )
```

```python
import jax
import jax.numpy as jnp
from jax import lax
from jax.experimental import pallas as pl
from jax.experimental.pallas import tpu as pltpu
from jax.sharding import PartitionSpec as P

GROUP = 8
HEAD = 128
BLOCK = 128
DOCS = 64
INV_ROOT = HEAD**-0.5
LOG2E = 1.4426950408889634
MASKED = -1e30
ALL = 60
BF = jnp.bfloat16
F32 = jnp.float32


def call(kernel, outs, n_in, smem=(), scratch=(), raw=False):
    place = pltpu.HBM if raw else pltpu.VMEM
    specs = [pl.BlockSpec(memory_space=pltpu.SMEM if i in smem else place) for i in range(n_in)]
    return pl.pallas_call(
        kernel,
        out_shape=[jax.ShapeDtypeStruct(*o) for o in outs],
        in_specs=specs,
        out_specs=[pl.BlockSpec(memory_space=pltpu.VMEM)] * len(outs),
        scratch_shapes=list(scratch),
        compiler_params=pltpu.CompilerParams(vmem_limit_bytes=(ALL if raw else 40) * 1024 * 1024),
    )


def fetch(sources, targets, sems):
    copies = [
        pltpu.make_async_copy(source, target, sems.at[i])
        for i, (source, target) in enumerate(zip(sources, targets))
    ]
    for copy in copies:
        copy.start()
    for copy in copies:
        copy.wait()


def two_terms(x):
    high = x.astype(BF)
    return high, (x - high.astype(F32)).astype(BF)


def pack_small(key_raw, value_raw, packed_ref, key_ref, value_ref, sems):
    fetch((key_raw, value_raw), (key_ref, value_ref), sems)
    for half in range(2):
        rows = pl.ds(half * 16, 16)
        for j in range(8):
            cols = pl.ds(j * HEAD, HEAD)
            packed_ref[j, rows, :HEAD] = key_ref[half, :, cols]
            packed_ref[j, rows, HEAD:] = value_ref[half, :, cols]


def pack_large(length_ref, *refs):
    packed_ref, start_ref, sems = refs[4], refs[5], refs[10]
    fetch(refs[:4], refs[6:10], sems)
    query_ref, grad_ref, out_ref, norm_ref = refs[6:10]
    heads = grad_ref.shape[2] // HEAD
    lane = lax.broadcasted_iota(jnp.int32, (16, heads), 1)
    source = lax.broadcasted_iota(jnp.int32, (4 * heads, HEAD), 0)
    target = lax.broadcasted_iota(jnp.int32, (4 * heads, HEAD), 1)
    offset = source - (lax.div(target, GROUP) * heads + lax.rem(target, GROUP))
    stats = []
    for half in range(2):
        delta = jnp.zeros((16, heads), F32)
        for n in range(heads):
            cols = pl.ds(n * HEAD, HEAD)
            product = out_ref[half, :, cols].astype(F32) * grad_ref[half, :, cols].astype(F32)
            delta = jnp.where(lane == n, jnp.sum(product, axis=1, keepdims=True), delta)
        stats.append(jnp.concatenate([*two_terms(norm_ref[half]), *two_terms(delta)], axis=1))
    stats = jnp.concatenate(stats, axis=0)
    for j in range(8):
        pick = jnp.where((offset == j * GROUP) & (target < 4 * GROUP), 1.0, 0.0).astype(BF)
        packed_ref[j, :, 2048:] = dot(stats, pick, (1, 0)).astype(BF)
        for half in range(2):
            rows = pl.ds(half * 16, 16)
            cols = pl.ds(j * 1024, 1024)
            packed_ref[j, rows, 0:1024] = query_ref[half, :, cols]
            packed_ref[j, rows, 1024:2048] = grad_ref[half, :, cols]
    ctx = lax.axis_index("ctx")
    row = lax.broadcasted_iota(jnp.int32, (8, BLOCK), 0)
    base = jnp.where(row == 0, ctx, 127 - ctx) * BLOCK
    position = base + lax.broadcasted_iota(jnp.int32, (8, BLOCK), 1)
    start = jnp.zeros((8, BLOCK), jnp.int32)
    end = jnp.int32(0)
    for j in range(DOCS):
        end = end + length_ref[j]
        start = jnp.where(position >= end, end, start)
    start_ref[...] = start - base


def unpack_small(packed_ref, own_ref, third_ref):
    odd = lax.rem(lax.axis_index("ctx"), 2) == 1
    low, high = (packed_ref[:, h : h + 16, :].reshape(BLOCK, 256) for h in (0, 16))
    own_ref[0] = low
    own_ref[1] = high
    third_ref[...] = jnp.where(odd, low, high)


def dot(a, b, contract):
    return lax.dot_general(a, b, ((contract[:1], contract[1:]), ((), ())), preferred_element_type=F32)


def pair_up(own_ref, mate_ref, first_out, second_out):
    ctx = lax.axis_index("ctx")
    odd = lax.rem(ctx, 2) == 1
    swapped = lax.rem(lax.div(ctx, 2), 2) == 1
    low, high = ((own_ref[h], mate_ref[h]) for h in range(2))
    low = [jnp.where(odd, low[s], low[1 - s]) for s in range(2)]
    high = [jnp.where(odd, high[1 - s], high[s]) for s in range(2)]
    for s in range(2):
        first_out[s] = jnp.where(swapped, high[s], low[s])
        second_out[s] = jnp.where(swapped, low[s], high[s])


def rows_of(half):
    return pl.ds(pl.multiple_of(half * 16, 16), 16)


def tile_gradients(rows_ref, stat_ref, start_ref, half, backs, tiles, put_query):
    key_at = lax.broadcasted_iota(jnp.int32, (BLOCK, BLOCK), 0)
    row_at = lax.broadcasted_iota(jnp.int32, (BLOCK, BLOCK), 1)
    start = start_ref[pl.ds(half, 1), :]
    allowed = [key_at - BLOCK * back >= start for back in backs]
    if backs[0] == 0:
        allowed[0] = allowed[0] & (key_at <= row_at)
    bias = jnp.concatenate([jnp.where(a, 0.0, MASKED) for a in allowed], axis=0)
    bias = jnp.concatenate([bias, bias], axis=1)
    keys = jnp.concatenate([t[:, :HEAD] for t in tiles], axis=0)
    values = jnp.concatenate([t[:, HEAD:] for t in tiles], axis=0)
    keys_turned = keys.T
    key_total = jnp.zeros(keys.shape, F32)
    value_total = jnp.zeros(keys.shape, F32)
    rows = rows_of(half)
    for g in range(0, GROUP, 2):

        def head_pair(offset):
            columns = [slice(offset + n * HEAD, offset + (n + 1) * HEAD) for n in (g, g + 1)]
            return jnp.concatenate([rows_ref[:, rows, c].reshape(BLOCK, HEAD) for c in columns], 0)

        query, grad = head_pair(0), head_pair(1024)
        norm, delta = (
            jnp.concatenate([stat_ref[half, s, n : n + 1, :] for n in (g, g + 1)], axis=1)
            for s in range(2)
        )
        scores = dot(keys, query, (1, 1))
        weights = jnp.exp2(scores * (INV_ROOT * LOG2E) - norm + bias)
        weight_grad = dot(values, grad, (1, 1))
        score_grad = (weights * (weight_grad - delta)).astype(BF)
        value_total += dot(weights.astype(BF), grad, (1, 0))
        key_total += dot(score_grad, query, (1, 0))
        put_query(g, dot(keys_turned, score_grad, (1, 0)))
    return key_total * INV_ROOT, value_total


def halves():
    even = 1 - lax.rem(lax.axis_index("ctx"), 2)
    return even, 1 - even


def near_gradients(
    rows_ref, own_ref, mate_ref, start_ref, turned, own_out, near_out, stat_ref, stat_turned
):
    for mated, half in zip((True, False), halves()):
        stats = rows_ref[:, rows_of(half), 2048:2176].reshape(BLOCK, HEAD)
        stat_turned[...] = stats.astype(F32).T
        stat_ref[half, 0] = (stat_turned[0:8, :] + stat_turned[8:16, :]) * LOG2E
        stat_ref[half, 1] = stat_turned[16:24, :] + stat_turned[24:32, :]

        def put(g, part):
            turned[half, :, g * HEAD : (g + 2) * HEAD] = part

        tiles, backs = [own_ref[half]], (0,)
        if mated:
            tiles, backs = tiles + [mate_ref[half]], (0, 1)
        key_total, value_total = tile_gradients(
            rows_ref, stat_ref, start_ref, half, backs, tiles, put
        )
        own_out[half, :, :HEAD] = key_total[:BLOCK]
        own_out[half, :, HEAD:] = value_total[:BLOCK]
        if mated:
            near_out[:, :HEAD] = key_total[BLOCK:].astype(BF)
            near_out[:, HEAD:] = value_total[BLOCK:].astype(BF)


def far_gradients(
    rows_ref, first_ref, second_ref, third_ref, stat_ref, start_ref, turned, near_ref,
    query_out, send_ref,
):
    ctx = lax.axis_index("ctx")
    member = lax.rem(ctx, 8)
    swapped = lax.rem(lax.div(ctx, 2), 2) == 1
    for mated, half in zip((True, False), halves()):
        from_first = swapped == (half == 0)
        tiles = [jnp.where(from_first, first_ref[s], second_ref[s]) for s in range(2)]
        backs = (2, 3)
        if not mated:
            tiles, backs = tiles + [third_ref[...]], (1, 2, 3)

        def put(g, part):
            part = (part + turned[half, :, g * HEAD : (g + 2) * HEAD]) * INV_ROOT
            for n in range(2):
                query_out[half, :, (g + n) * HEAD : (g + n + 1) * HEAD] = (
                    part[:, n * HEAD : (n + 1) * HEAD].T.astype(BF)
                )

        key_total, value_total = tile_gradients(
            rows_ref, stat_ref, start_ref, half, backs, tiles, put
        )

        def slot(back):
            return lax.rem(member + jnp.where(half == 1, back, 8 - back), 8)

        if mated:
            send_ref[slot(1)] = near_ref[...]
        for s, back in enumerate(backs):
            part = slice(s * BLOCK, (s + 1) * BLOCK)
            send_ref[slot(back), :, :HEAD] = key_total[part].astype(BF)
            send_ref[slot(back), :, HEAD:] = value_total[part].astype(BF)
    for apart in (0, 4):
        send_ref[lax.rem(member + apart, 8)] = jnp.zeros((BLOCK, 2 * HEAD), BF)


def add_group(own_ref, got_ref, sum_ref, pass_ref):
    member = lax.rem(lax.axis_index("ctx"), 8)
    zero = jnp.zeros((BLOCK, 2 * HEAD), F32)
    low, high, other = own_ref[0], own_ref[1], zero
    for s in range(8):
        got = got_ref[s].astype(F32)
        apart = lax.rem(s - member + 8, 8)
        from_low = (apart >= 1) & (apart <= 3)
        from_high = apart >= 5
        low = low + jnp.where(from_low & (s > member), got, 0.0)
        high = high + jnp.where(from_high & (s < member), got, 0.0)
        other = other + jnp.where((from_low & (s < member)) | (from_high & (s > member)), got, 0.0)
    sum_ref[0] = low
    sum_ref[1] = high
    pass_ref[...] = other.astype(BF)


def add_rest(sum_ref, got_ref, key_out, value_out):
    odd = lax.rem(lax.div(lax.axis_index("ctx"), 4), 2) == 1
    got = got_ref[...].astype(F32)
    for half in range(2):
        pick = odd if half == 0 else jnp.logical_not(odd)
        total = sum_ref[half] + jnp.where(pick, got, 0.0)
        key_out[half] = total[:, :HEAD].astype(BF)
        value_out[half] = total[:, HEAD:].astype(BF)


def between_groups():
    pairs = []
    for x in range(4):
        pairs += [(4 * z + x, 4 * (z + 2) + x) for z in range(0, 13, 2)]
        pairs += [(4 * z + x, 4 * (z - 2) + x) for z in range(3, 16, 2)]
        pairs += [(56 + x, 63 - x)]
    return pairs


def body(lengths, queries, keys, values, outputs, grads, norms):
    count = lax.axis_size("ctx")
    mates = [(i, i ^ 1) for i in range(count)]
    first_step = [(i, i ^ 2) for i in range(count)]
    second_step = [(i, i + 2 if i % 4 >= 2 else i - 2) for i in range(2, count - 2)]
    second_step += [(i, i) for i in (count - 2, count - 1)]
    third_step = [(i, i + 3) for i in range(1, count - 3, 2)]
    third_step += [(j, i) for i, j in third_step] + [(count - 3, count - 1), (count - 1, count - 3)]
    groups = [[8 * m + j for j in range(8)] for m in range(8)]

    def by_head(x):
        return lax.all_to_all(x, "kvh", split_axis=0, concat_axis=0, tiled=True)

    (small,) = call(
        pack_small,
        [((8, 32, 256), BF)],
        2,
        scratch=[pltpu.VMEM((2, 16, 1024), BF)] * 2 + [pltpu.SemaphoreType.DMA((2,))],
        raw=True,
    )(keys, values)
    small = by_head(small)
    large, starts = call(
        pack_large,
        [((8, 32, 2176), BF), ((8, BLOCK), jnp.int32)],
        5,
        smem=(0,),
        scratch=[pltpu.VMEM((2, 16, 8192), BF)] * 3
        + [pltpu.VMEM((2, 16, 64), F32), pltpu.SemaphoreType.DMA((4,))],
        raw=True,
    )(lengths, queries, grads, outputs, norms)
    large = by_head(large)
    tile = ((BLOCK, 256), BF)
    pair = ((2, BLOCK, 256), BF)
    held, third = call(unpack_small, [pair, tile], 1)(small)
    mate = lax.ppermute(held, "ctx", mates)
    third = lax.ppermute(third, "ctx", third_step)
    first, second = call(pair_up, [pair, pair], 2)(held, mate)
    first = lax.ppermute(first, "ctx", first_step)
    second = lax.ppermute(second, "ctx", second_step)
    turned, own, near, stats = call(
        near_gradients,
        [
            ((2, HEAD, 1024), F32),
            ((2, BLOCK, 256), F32),
            tile,
            ((2, 2, GROUP, BLOCK), F32),
        ],
        4,
        scratch=[pltpu.VMEM((HEAD, BLOCK), F32)],
    )(large, held, mate, starts)
    query_grad, sent = call(
        far_gradients, [((2, BLOCK, 1024), BF), ((8, BLOCK, 256), BF)], 8
    )(large, first, second, third, stats, starts, turned, near)
    got = lax.all_to_all(
        sent, "ctx", split_axis=0, concat_axis=0, tiled=True, axis_index_groups=groups
    )
    sums, passed = call(add_group, [((2, BLOCK, 256), F32), tile], 2)(own, got)
    passed = lax.ppermute(passed, "ctx", between_groups())
    key_grad, value_grad = call(add_rest, [((2, BLOCK, HEAD), BF)] * 2, 2)(sums, passed)
    return query_grad, key_grad, value_grad


def solution(mesh):
    rows = P(None, ("ctx", "kvh"), None)
    heads = P(None, "ctx", "kvh")
    return jax.shard_map(
        body,
        mesh=mesh,
        in_specs=(P(),) + (rows,) * 6,
        out_specs=(heads,) * 3,
        check_vma=False,
    )
```

```python
import jax
import jax.numpy as jnp
from jax import lax
from jax.experimental import pallas as pl
from jax.experimental.pallas import tpu as pltpu
from jax.sharding import PartitionSpec as P

GROUP = 8
HEAD = 128
BLOCK = 128
DOCS = 64
INV_ROOT = HEAD**-0.5
LOG2E = 1.4426950408889634
MASKED = -1e30
ALL = 60
BF = jnp.bfloat16
F32 = jnp.float32


def call(kernel, outs, n_in, smem=(), scratch=(), raw=False):
    place = pltpu.HBM if raw else pltpu.VMEM
    specs = [pl.BlockSpec(memory_space=pltpu.SMEM if i in smem else place) for i in range(n_in)]
    return pl.pallas_call(
        kernel,
        out_shape=[jax.ShapeDtypeStruct(*o) for o in outs],
        in_specs=specs,
        out_specs=[pl.BlockSpec(memory_space=pltpu.VMEM)] * len(outs),
        scratch_shapes=list(scratch),
        compiler_params=pltpu.CompilerParams(vmem_limit_bytes=(ALL if raw else 40) * 1024 * 1024),
    )


def fetch(sources, targets, sems):
    copies = [
        pltpu.make_async_copy(source, target, sems.at[i])
        for i, (source, target) in enumerate(zip(sources, targets))
    ]
    for copy in copies:
        copy.start()
    for copy in copies:
        copy.wait()


def two_terms(x):
    high = x.astype(BF)
    return high, (x - high.astype(F32)).astype(BF)


def pack_small(key_raw, value_raw, packed_ref, key_ref, value_ref, sems):
    fetch((key_raw, value_raw), (key_ref, value_ref), sems)
    for half in range(2):
        rows = pl.ds(half * 16, 16)
        for j in range(8):
            cols = pl.ds(j * HEAD, HEAD)
            packed_ref[j, rows, :HEAD] = key_ref[half, :, cols]
            packed_ref[j, rows, HEAD:] = value_ref[half, :, cols]


def pack_large(length_ref, *refs):
    packed_ref, start_ref, sems = refs[4], refs[5], refs[10]
    fetch(refs[:4], refs[6:10], sems)
    query_ref, grad_ref, out_ref, norm_ref = refs[6:10]
    heads = grad_ref.shape[2] // HEAD
    lane = lax.broadcasted_iota(jnp.int32, (16, heads), 1)
    source = lax.broadcasted_iota(jnp.int32, (4 * heads, HEAD), 0)
    target = lax.broadcasted_iota(jnp.int32, (4 * heads, HEAD), 1)
    offset = source - (lax.div(target, GROUP) * heads + lax.rem(target, GROUP))
    stats = []
    for half in range(2):
        delta = jnp.zeros((16, heads), F32)
        for n in range(heads):
            cols = pl.ds(n * HEAD, HEAD)
            product = out_ref[half, :, cols].astype(F32) * grad_ref[half, :, cols].astype(F32)
            delta = jnp.where(lane == n, jnp.sum(product, axis=1, keepdims=True), delta)
        stats.append(jnp.concatenate([*two_terms(norm_ref[half]), *two_terms(delta)], axis=1))
    stats = jnp.concatenate(stats, axis=0)
    for j in range(8):
        pick = jnp.where((offset == j * GROUP) & (target < 4 * GROUP), 1.0, 0.0).astype(BF)
        packed_ref[j, :, 2048:] = dot(stats, pick, (1, 0)).astype(BF)
        for half in range(2):
            rows = pl.ds(half * 16, 16)
            cols = pl.ds(j * 1024, 1024)
            packed_ref[j, rows, 0:1024] = query_ref[half, :, cols]
            packed_ref[j, rows, 1024:2048] = grad_ref[half, :, cols]
    ctx = lax.axis_index("ctx")
    row = lax.broadcasted_iota(jnp.int32, (8, BLOCK), 0)
    base = jnp.where(row == 0, ctx, 127 - ctx) * BLOCK
    position = base + lax.broadcasted_iota(jnp.int32, (8, BLOCK), 1)
    start = jnp.zeros((8, BLOCK), jnp.int32)
    end = jnp.int32(0)
    for j in range(DOCS):
        end = end + length_ref[j]
        start = jnp.where(position >= end, end, start)
    start_ref[...] = start - base


def unpack_small(packed_ref, own_ref, third_ref):
    odd = lax.rem(lax.axis_index("ctx"), 2) == 1
    low, high = (packed_ref[:, h : h + 16, :].reshape(BLOCK, 256) for h in (0, 16))
    own_ref[0] = low
    own_ref[1] = high
    third_ref[...] = jnp.where(odd, low, high)


def dot(a, b, contract):
    return lax.dot_general(a, b, ((contract[:1], contract[1:]), ((), ())), preferred_element_type=F32)


def pair_up(own_ref, mate_ref, first_out, second_out):
    ctx = lax.axis_index("ctx")
    odd = lax.rem(ctx, 2) == 1
    swapped = lax.rem(lax.div(ctx, 2), 2) == 1
    low, high = ((own_ref[h], mate_ref[h]) for h in range(2))
    low = [jnp.where(odd, low[s], low[1 - s]) for s in range(2)]
    high = [jnp.where(odd, high[1 - s], high[s]) for s in range(2)]
    for s in range(2):
        first_out[s] = jnp.where(swapped, high[s], low[s])
        second_out[s] = jnp.where(swapped, low[s], high[s])


def rows_of(half):
    return pl.ds(pl.multiple_of(half * 16, 16), 16)


def tile_gradients(rows_ref, stat_ref, start_ref, half, backs, tiles, put_scores):
    key_at = lax.broadcasted_iota(jnp.int32, (BLOCK, BLOCK), 0)
    row_at = lax.broadcasted_iota(jnp.int32, (BLOCK, BLOCK), 1)
    start = start_ref[pl.ds(half, 1), :]
    allowed = [key_at - BLOCK * back >= start for back in backs]
    if backs[0] == 0:
        allowed[0] = allowed[0] & (key_at <= row_at)
    bias = jnp.concatenate([jnp.where(a, 0.0, MASKED) for a in allowed], axis=0)
    bias = jnp.concatenate([bias, bias], axis=1)
    keys = jnp.concatenate([t[:, :HEAD] for t in tiles], axis=0)
    values = jnp.concatenate([t[:, HEAD:] for t in tiles], axis=0)
    keys_turned = keys.T
    key_total = jnp.zeros(keys.shape, F32)
    value_total = jnp.zeros(keys.shape, F32)
    rows = rows_of(half)
    for g in range(0, GROUP, 2):

        def head_pair(offset):
            columns = [slice(offset + n * HEAD, offset + (n + 1) * HEAD) for n in (g, g + 1)]
            return jnp.concatenate([rows_ref[:, rows, c].reshape(BLOCK, HEAD) for c in columns], 0)

        query, grad = head_pair(0), head_pair(1024)
        norm, delta = (
            jnp.concatenate([stat_ref[half, s, n : n + 1, :] for n in (g, g + 1)], axis=1)
            for s in range(2)
        )
        scores = dot(keys, query, (1, 1))
        weights = jnp.exp2(scores * (INV_ROOT * LOG2E) - norm + bias)
        weight_grad = dot(values, grad, (1, 1))
        score_grad = (weights * (weight_grad - delta)).astype(BF)
        value_total += dot(weights.astype(BF), grad, (1, 0))
        key_total += dot(score_grad, query, (1, 0))
        put_scores(g, score_grad, keys_turned)
    return key_total * INV_ROOT, value_total


def halves():
    even = 1 - lax.rem(lax.axis_index("ctx"), 2)
    return even, 1 - even


def near_gradients(
    rows_ref, own_ref, mate_ref, start_ref, turned, own_out, near_out, stat_ref, stat_turned
):
    for mated, half in zip((True, False), halves()):
        stats = rows_ref[:, rows_of(half), 2048:2176].reshape(BLOCK, HEAD)
        stat_turned[...] = stats.astype(F32).T
        stat_ref[half, 0] = (stat_turned[0:8, :] + stat_turned[8:16, :]) * LOG2E
        stat_ref[half, 1] = stat_turned[16:24, :] + stat_turned[24:32, :]

        tiles, backs = [own_ref[half]], (0,)
        if mated:
            tiles, backs = tiles + [mate_ref[half]], (0, 1)

        def put(g, scores, keys_turned):
            turned[half, :, g * HEAD : (g + 2) * HEAD] = dot(keys_turned, scores, (1, 0))

        key_total, value_total = tile_gradients(
            rows_ref, stat_ref, start_ref, half, backs, tiles, put
        )
        own_out[half, :, :HEAD] = key_total[:BLOCK]
        own_out[half, :, HEAD:] = value_total[:BLOCK]
        if mated:
            near_out[:, :HEAD] = key_total[BLOCK:].astype(BF)
            near_out[:, HEAD:] = value_total[BLOCK:].astype(BF)


def far_tiles(first_ref, second_ref, third_ref, mated, half):
    swapped = lax.rem(lax.div(lax.axis_index("ctx"), 2), 2) == 1
    from_first = swapped == (half == 0)
    tiles = [jnp.where(from_first, first_ref[s], second_ref[s]) for s in range(2)]
    return (tiles, (2, 3)) if mated else (tiles + [third_ref[...]], (1, 2, 3))


def far_gradients(
    rows_ref, first_ref, second_ref, third_ref, stat_ref, start_ref, near_ref,
    score_out, send_ref,
):
    member = lax.rem(lax.axis_index("ctx"), 8)
    for mated, half in zip((True, False), halves()):
        tiles, backs = far_tiles(first_ref, second_ref, third_ref, mated, half)
        keys_at = slice(0, 2 * BLOCK) if mated else slice(2 * BLOCK, 5 * BLOCK)

        def put(g, scores, keys_turned):
            score_out[keys_at, g * HEAD : (g + 2) * HEAD] = scores

        key_total, value_total = tile_gradients(
            rows_ref, stat_ref, start_ref, half, backs, tiles, put
        )

        def slot(back):
            return lax.rem(member + jnp.where(half == 1, back, 8 - back), 8)

        if mated:
            send_ref[slot(1)] = near_ref[...]
        for s, back in enumerate(backs):
            part = slice(s * BLOCK, (s + 1) * BLOCK)
            send_ref[slot(back), :, :HEAD] = key_total[part].astype(BF)
            send_ref[slot(back), :, HEAD:] = value_total[part].astype(BF)
    for apart in (0, 4):
        send_ref[lax.rem(member + apart, 8)] = jnp.zeros((BLOCK, 2 * HEAD), BF)


def query_gradients(first_ref, second_ref, third_ref, score_ref, turned, query_out):
    for mated, half in zip((True, False), halves()):
        tiles, _ = far_tiles(first_ref, second_ref, third_ref, mated, half)
        keys_at = slice(0, 2 * BLOCK) if mated else slice(2 * BLOCK, 5 * BLOCK)
        keys_turned = jnp.concatenate([t[:, :HEAD] for t in tiles], axis=0).T
        for g in range(0, GROUP, 2):
            columns = slice(g * HEAD, (g + 2) * HEAD)
            part = dot(keys_turned, score_ref[keys_at, columns], (1, 0))
            part = (part + turned[half, :, columns]) * INV_ROOT
            for n in range(2):
                query_out[half, :, (g + n) * HEAD : (g + n + 1) * HEAD] = (
                    part[:, n * HEAD : (n + 1) * HEAD].T.astype(BF)
                )


def add_group(own_ref, got_ref, sum_ref, pass_ref):
    member = lax.rem(lax.axis_index("ctx"), 8)
    zero = jnp.zeros((BLOCK, 2 * HEAD), F32)
    low, high, other = own_ref[0], own_ref[1], zero
    for s in range(8):
        got = got_ref[s].astype(F32)
        apart = lax.rem(s - member + 8, 8)
        from_low = (apart >= 1) & (apart <= 3)
        from_high = apart >= 5
        low = low + jnp.where(from_low & (s > member), got, 0.0)
        high = high + jnp.where(from_high & (s < member), got, 0.0)
        other = other + jnp.where((from_low & (s < member)) | (from_high & (s > member)), got, 0.0)
    sum_ref[0] = low
    sum_ref[1] = high
    pass_ref[...] = other.astype(BF)


def add_rest(sum_ref, got_ref, key_out, value_out):
    odd = lax.rem(lax.div(lax.axis_index("ctx"), 4), 2) == 1
    got = got_ref[...].astype(F32)
    for half in range(2):
        pick = odd if half == 0 else jnp.logical_not(odd)
        total = sum_ref[half] + jnp.where(pick, got, 0.0)
        key_out[half] = total[:, :HEAD].astype(BF)
        value_out[half] = total[:, HEAD:].astype(BF)


def between_groups():
    pairs = []
    for x in range(4):
        pairs += [(4 * z + x, 4 * (z + 2) + x) for z in range(0, 13, 2)]
        pairs += [(4 * z + x, 4 * (z - 2) + x) for z in range(3, 16, 2)]
        pairs += [(56 + x, 63 - x)]
    return pairs


def body(lengths, queries, keys, values, outputs, grads, norms):
    count = lax.axis_size("ctx")
    mates = [(i, i ^ 1) for i in range(count)]
    first_step = [(i, i ^ 2) for i in range(count)]
    second_step = [(i, i + 2 if i % 4 >= 2 else i - 2) for i in range(2, count - 2)]
    second_step += [(i, i) for i in (count - 2, count - 1)]
    third_step = [(i, i + 3) for i in range(1, count - 3, 2)]
    third_step += [(j, i) for i, j in third_step] + [(count - 3, count - 1), (count - 1, count - 3)]
    groups = [[8 * m + j for j in range(8)] for m in range(8)]

    def by_head(x):
        return lax.all_to_all(x, "kvh", split_axis=0, concat_axis=0, tiled=True)

    (small,) = call(
        pack_small,
        [((8, 32, 256), BF)],
        2,
        scratch=[pltpu.VMEM((2, 16, 1024), BF)] * 2 + [pltpu.SemaphoreType.DMA((2,))],
        raw=True,
    )(keys, values)
    small = by_head(small)
    large, starts = call(
        pack_large,
        [((8, 32, 2176), BF), ((8, BLOCK), jnp.int32)],
        5,
        smem=(0,),
        scratch=[pltpu.VMEM((2, 16, 8192), BF)] * 3
        + [pltpu.VMEM((2, 16, 64), F32), pltpu.SemaphoreType.DMA((4,))],
        raw=True,
    )(lengths, queries, grads, outputs, norms)
    large = by_head(large)
    tile = ((BLOCK, 256), BF)
    pair = ((2, BLOCK, 256), BF)
    held, third = call(unpack_small, [pair, tile], 1)(small)
    mate = lax.ppermute(held, "ctx", mates)
    third = lax.ppermute(third, "ctx", third_step)
    first, second = call(pair_up, [pair, pair], 2)(held, mate)
    first = lax.ppermute(first, "ctx", first_step)
    second = lax.ppermute(second, "ctx", second_step)
    turned, own, near, stats = call(
        near_gradients,
        [
            ((2, HEAD, 1024), F32),
            ((2, BLOCK, 256), F32),
            tile,
            ((2, 2, GROUP, BLOCK), F32),
        ],
        4,
        scratch=[pltpu.VMEM((HEAD, BLOCK), F32)],
    )(large, held, mate, starts)
    scores, sent = call(
        far_gradients, [((5 * BLOCK, 1024), BF), ((8, BLOCK, 256), BF)], 7
    )(large, first, second, third, stats, starts, near)
    got = lax.all_to_all(
        sent, "ctx", split_axis=0, concat_axis=0, tiled=True, axis_index_groups=groups
    )
    (query_grad,) = call(query_gradients, [((2, BLOCK, 1024), BF)], 5)(
        first, second, third, scores, turned
    )
    sums, passed = call(add_group, [((2, BLOCK, 256), F32), tile], 2)(own, got)
    passed = lax.ppermute(passed, "ctx", between_groups())
    key_grad, value_grad = call(add_rest, [((2, BLOCK, HEAD), BF)] * 2, 2)(sums, passed)
    return query_grad, key_grad, value_grad


def solution(mesh):
    rows = P(None, ("ctx", "kvh"), None)
    heads = P(None, "ctx", "kvh")
    return jax.shard_map(
        body,
        mesh=mesh,
        in_specs=(P(),) + (rows,) * 6,
        out_specs=(heads,) * 3,
        check_vma=False,
    )
```
